256 devices in a mesh: dp: 128 (over x, y, z), helper: 2 (over core).
Axes of the slice: x: 4, y: 4, z: 8, core: 2. Of those that a mesh axis runs over, the one named last changes fastest.
Arguments:
- embedding: bfloat16 [98304, 1024], P(('dp', 'helper'))
- cluster: int32 [98304], P(('dp', 'helper')), may hold values from 0 to 511, as said below
- member_order: int32 [98304], P(('dp', 'helper')), may hold values from 0 to 98303, each once
Outputs:
- nearest: float32 [98304], P(('dp', 'helper'))
The draws below stay inside these ranges and needn't reach their ends.
Inputs may be any that keep to these rules, and one draw needn't show every extreme that they name: The owner of a cluster c is c mod 128; among the documents of one device at most 6 have the same owner, and on every device some owner has exactly 6. `member_order`: each value appears once.
All inputs are finite; a program needn't handle non-finite values.
Results may differ from the reference program's by a relative error of at most 0.0005.
Values may be sent and summed in bfloat16 or wider, within the bound.
No kernel may reach another device: no remote copies, remote signals or barrier semaphores. Data moves between devices by JAX's collectives and lax.ppermute only.
A program may use at most 64 MiB of HBM per device.

```python
import math
import jax
import jax.numpy as jnp
from jax import lax

D = 1024
R_DEV = 384
CL_OWN = 4
CAP = 6
ROWS = 98304
N_DP = 128
N_HELPER = 2


def cluster_plan(key):
    popular = jax.random.randint(jax.random.fold_in(key, 11), (N_DP,), 0, 4)
    slot_total = N_DP * CAP

    def one_device(device_key):
        key_force, key_score, key_shuffle, key_member = jax.random.split(device_key, 4)
        forced = jax.random.randint(key_force, (), 0, N_DP)
        slot_ids = jnp.arange(slot_total, dtype=jnp.int32)
        holder = slot_ids // CAP
        jitter = jax.random.randint(key_score, (slot_total,), 0, 2 ** 16)
        ranking = (jitter + (3 - popular[holder]) * 2 ** 16 + 1) * slot_total + slot_ids
        ranking = jnp.where(holder == forced, slot_ids, ranking)
        picked = jnp.argsort(ranking, stable=True)[:R_DEV]
        chosen = holder[picked]
        chosen = chosen[jax.random.permutation(key_shuffle, R_DEV)]
        member = jax.random.randint(key_member, (R_DEV,), 0, CL_OWN)
        return member * N_DP + chosen
    device_keys = jax.random.split(jax.random.fold_in(key, 12), ROWS // R_DEV)
    return jax.vmap(one_device)(device_keys).reshape(-1).astype(jnp.int32)


def draw_cluster(key, part):
    labels = cluster_plan(key)
    return labels


def draw_embedding(key, part):
    labels = cluster_plan(key)
    key = jax.random.fold_in(key, 5)
    key_center, key_spread, key_noise = jax.random.split(key, 3)
    centers = jax.random.normal(key_center, (CL_OWN * N_DP, D), jnp.float32)
    spread = jnp.exp(jax.random.uniform(key_spread, (ROWS, 1), jnp.float32, math.log(0.3), math.log(2.0)))
    noise = jax.random.normal(key_noise, (ROWS, D), jnp.float32)
    values = centers[labels] * spread + noise
    return values.astype(jnp.bfloat16)


def setup_inputs(seed: int = 0) -> dict:
    keys = jax.random.split(jax.random.key(seed), 4)
    return {
        "embedding": draw_embedding(jax.random.fold_in(keys[3], 71), 0),
        "cluster": draw_cluster(jax.random.fold_in(keys[3], 71), 0),
        "member_order": jax.random.permutation(keys[2], ROWS).astype(jnp.int32),
    }


def normalize(embedding):
    values = embedding.astype(jnp.float32)
    return (values * lax.rsqrt(lax.optimization_barrier(jnp.sum(values * values, axis=1, keepdims=True)) + 1e-06)).astype(jnp.bfloat16)

def reference(embedding, cluster, member_order):
    normed = normalize(embedding)
    owner = cluster % N_DP
    slot_total = N_DP * N_HELPER * CAP
    row_total = cluster.shape[0]

    def per_owner(carry, target):
        outside = (owner != target).astype(jnp.int32)
        picked = jnp.argsort(outside, stable=True)[:slot_total].astype(jnp.int32)
        present = owner[picked] == target
        rows_here = normed[picked]
        group = jnp.where(present, cluster[picked], -1)
        ranks = member_order[picked]
        scores = jnp.dot(rows_here, rows_here.T, preferred_element_type=jnp.float32)
        allowed = (group[:, None] == group[None, :]) & (ranks[None, :] < ranks[:, None]) & (group[None, :] >= 0)
        best_here = lax.optimization_barrier(jnp.max(jnp.where(allowed, scores, -1.0), axis=1))
        updated = carry.at[picked].set(jnp.where(present, best_here, carry[picked]))
        return (updated, None)
    start_best = jnp.full((row_total,), -1.0, jnp.float32)
    result, _ = lax.scan(per_owner, start_best, jnp.arange(N_DP, dtype=jnp.int32))
    return result
```

```python
import functools

import jax
import jax.numpy as jnp
from jax import lax
from jax.experimental import pallas as pl
from jax.experimental.pallas import tpu as pltpu
from jax.sharding import PartitionSpec as P

LANES = 128
META = 8
CLASS = 1 << 17
VMEM_LIMIT = 48 << 20


def routing(cluster, owners):
    count = cluster.shape[1]
    owner = lax.rem(cluster, owners)
    member = lax.broadcasted_iota(jnp.int32, (owners, count), 0) == owner
    before = lax.broadcasted_iota(jnp.int32, (count, count), 0) < lax.broadcasted_iota(
        jnp.int32, (count, count), 1
    )
    ones = member.astype(jnp.bfloat16)
    earlier = jnp.dot(ones, before.astype(jnp.bfloat16), preferred_element_type=jnp.float32)
    slot = jnp.sum(jnp.where(member, earlier, 0.0), axis=0, keepdims=True).astype(jnp.int32)
    return member, slot


def pack_kernel(owners, cap, cluster_ref, order_ref, x_ref, out_ref, wide):
    chunks = x_ref.shape[1] // LANES
    block = cap * chunks + META
    cluster = cluster_ref[...]
    order = order_ref[...]
    member, slot = routing(cluster, owners)
    values = x_ref[...].astype(jnp.float32)
    scale = lax.rsqrt(jnp.sum(values * values, axis=1, keepdims=True) + 1e-06)
    normed = (values * scale).astype(jnp.bfloat16)
    for s in range(cap):
        pick = (member & (slot == s)).astype(jnp.bfloat16)
        rows = jnp.dot(pick, normed, preferred_element_type=jnp.float32)
        for j in range(chunks):
            wide[pl.ds(s * chunks + j, owners, stride=block), :] = rows[
                :, j * LANES : (j + 1) * LANES
            ]
    ones = member.astype(jnp.bfloat16)
    place = lax.broadcasted_iota(jnp.int32, (LANES, cluster.shape[1]), 0) == slot
    digits = (order & 255, (order >> 8) & 255, (order >> 16) + 2 * lax.div(cluster, owners) + 8)
    for r in range(META):
        if r < len(digits):
            spread = jnp.where(place, digits[r].astype(jnp.float32), 0.0).astype(jnp.bfloat16)
            rows = lax.dot_general(
                ones, spread, (((1,), (1,)), ((), ())), preferred_element_type=jnp.float32
            )
        else:
            rows = jnp.zeros((owners, LANES), jnp.float32)
        wide[pl.ds(cap * chunks + r, owners, stride=block), :] = rows
    out_ref[...] = wide[...].astype(jnp.bfloat16)


def unpack(sources, cap, block_ref, wide, rows_ref):
    chunks = rows_ref.shape[1] // LANES
    block = cap * chunks + META
    wide[...] = block_ref[...].astype(jnp.float32)
    for s in range(cap):
        for j in range(chunks):
            rows_ref[s * sources : (s + 1) * sources, j * LANES : (j + 1) * LANES] = wide[
                pl.ds(s * chunks + j, sources, stride=block), :
            ].astype(jnp.bfloat16)
    digit = [wide[pl.ds(cap * chunks + r, sources, stride=block), :] for r in range(3)]
    return (digit[0] + 256.0 * digit[1] + 65536.0 * digit[2]).astype(jnp.int32)


def best_of(sources, cap, keys_ref, key_value, queries_ref, query_value, best_ref):
    turned = query_value.T
    for q in range(cap):
        mine = turned[q : q + 1, :]
        floor = mine & ~(CLASS - 1)
        best = best_ref[q : q + 1, :]
        queries = queries_ref[q * sources : (q + 1) * sources, :]
        for k in range(cap):
            scores = lax.dot_general(
                keys_ref[k * sources : (k + 1) * sources, :],
                queries,
                (((1,), (1,)), ((), ())),
                preferred_element_type=jnp.float32,
            )
            theirs = key_value[:, k : k + 1]
            allowed = (theirs >= floor) & (theirs < mine)
            best = jnp.maximum(
                best, jnp.max(jnp.where(allowed, scores, -1.0), axis=0, keepdims=True)
            )
        best_ref[q : q + 1, :] = best


def own_kernel(sources, cap, block_ref, rows_ref, value_ref, best_ref, wide):
    value = unpack(sources, cap, block_ref, wide, rows_ref)
    value_ref[...] = value
    best_ref[...] = jnp.full(best_ref.shape, -1.0, jnp.float32)
    best_of(sources, cap, rows_ref, value, rows_ref, value, best_ref)


def other_kernel(
    sources, cap, block_ref, own_ref, own_value_ref, own_best_ref, out_ref, wide, rows, best
):
    value = unpack(sources, cap, block_ref, wide, rows)
    best[...] = jnp.full(best.shape, -1.0, jnp.float32)
    best[: own_best_ref.shape[0], :] = own_best_ref[...]
    best_of(sources, cap, rows, value, own_ref, own_value_ref[...], best)
    out_ref[...] = best[...].T


def pick_kernel(owners, cap, cluster_ref, result_ref, out_ref):
    member, slot = routing(cluster_ref[...], owners)
    result = result_ref[...]
    found = jnp.full(slot.shape, -1.0, jnp.float32)
    for s in range(cap):
        here = jnp.max(
            jnp.where(member, result[:, s : s + 1], -2.0), axis=0, keepdims=True
        )
        found = jnp.where(slot == s, here, found)
    out_ref[...] = found


def call(kernel, out_shape, scratch=()):
    return pl.pallas_call(
        kernel,
        out_shape=out_shape,
        scratch_shapes=list(scratch),
        compiler_params=pltpu.CompilerParams(vmem_limit_bytes=VMEM_LIMIT),
    )


def per_device(embedding, cluster, member_order):
    owners = lax.axis_size("dp")
    count, feature = embedding.shape
    cap = max(2, 2 * count // owners)
    block = cap * feature // LANES + META
    cluster = cluster.reshape(1, count)
    order = member_order.reshape(1, count)
    shape = jax.ShapeDtypeStruct
    wide = pltpu.VMEM((owners * block, LANES), jnp.float32)
    packed = call(
        functools.partial(pack_kernel, owners, cap),
        shape((owners * block, LANES), jnp.bfloat16),
        [wide],
    )(cluster, order, embedding)
    arrived = lax.all_to_all(
        packed.reshape(owners, block, LANES), "dp", split_axis=0, concat_axis=0, tiled=True
    ).reshape(owners * block, LANES)
    other = lax.ppermute(arrived, "helper", [(0, 1), (1, 0)])
    rows, value, best = call(
        functools.partial(own_kernel, owners, cap),
        (
            shape((owners * cap, feature), jnp.bfloat16),
            shape((owners, LANES), jnp.int32),
            shape((8, owners), jnp.float32),
        ),
        [wide],
    )(arrived)
    nearest = call(
        functools.partial(other_kernel, owners, cap),
        shape((owners, LANES), jnp.float32),
        [
            wide,
            pltpu.VMEM((owners * cap, feature), jnp.bfloat16),
            pltpu.VMEM((LANES, owners), jnp.float32),
        ],
    )(other, rows, value, best)
    returned = lax.all_to_all(
        nearest.reshape(owners, 1, LANES), "dp", split_axis=0, concat_axis=0, tiled=True
    ).reshape(owners, LANES)
    found = call(
        functools.partial(pick_kernel, owners, cap), shape((1, count), jnp.float32)
    )(cluster, returned)
    return found.reshape(count)


def solution(mesh):
    in_specs = (P(("dp", "helper"), None), P(("dp", "helper")), P(("dp", "helper")))
    out_specs = P(("dp", "helper"))
    return jax.shard_map(
        per_device, mesh=mesh, in_specs=in_specs, out_specs=out_specs, check_vma=False
    )
```

```python
import functools

import jax
import jax.numpy as jnp
from jax import lax
from jax.experimental import pallas as pl
from jax.experimental.pallas import tpu as pltpu
from jax.sharding import PartitionSpec as P

LANES = 128
META = 2
SIDE = 8
CLASS = 1 << 17
VMEM_LIMIT = 48 << 20


def routing(cluster, owners):
    count = cluster.shape[1]
    owner = lax.rem(cluster, owners)
    member = lax.broadcasted_iota(jnp.int32, (owners, count), 0) == owner
    before = lax.broadcasted_iota(jnp.int32, (count, count), 0) < lax.broadcasted_iota(
        jnp.int32, (count, count), 1
    )
    ones = member.astype(jnp.bfloat16)
    earlier = jnp.dot(ones, before.astype(jnp.bfloat16), preferred_element_type=jnp.float32)
    slot = jnp.sum(jnp.where(member, earlier, 0.0), axis=0, keepdims=True).astype(jnp.int32)
    return member, slot


def pack_kernel(
    owners, cap, cluster_hbm, order_hbm, x_hbm, out_ref, cluster_ref, order_ref, x_ref, wide, arrived
):
    given = (cluster_hbm, order_hbm, x_hbm)
    fetch = [
        pltpu.make_async_copy(source, target, arrived.at[i])
        for i, (source, target) in enumerate(zip(given, (cluster_ref, order_ref, x_ref)))
    ]
    for copy in fetch:
        copy.start()
    fetch[0].wait()
    fetch[1].wait()
    count, feature = x_ref.shape
    chunks = feature // LANES
    block = cap * chunks + META
    cluster = cluster_ref[...].reshape(1, count)
    order = order_ref[...].reshape(1, count)
    member, slot = routing(cluster, owners)
    ones = member.astype(jnp.bfloat16)
    lane = lax.broadcasted_iota(jnp.int32, (LANES, count), 0)
    low, middle = order & 255, (order >> 8) & 255
    high = (order >> 16) + 2 * lax.div(cluster, owners) + 8
    spread = (
        jnp.where(lane == slot, low, jnp.where(lane == slot + SIDE, middle, 0)),
        jnp.where(lane == slot, high, 0),
    )
    for r in range(META):
        wide[pl.ds(cap * chunks + r, owners, stride=block), :] = lax.dot_general(
            ones,
            spread[r].astype(jnp.float32).astype(jnp.bfloat16),
            (((1,), (1,)), ((), ())),
            preferred_element_type=jnp.float32,
        )
    fetch[2].wait()
    values = x_ref[...].astype(jnp.float32)
    scale = lax.rsqrt(jnp.sum(values * values, axis=1, keepdims=True) + 1e-06)
    normed = (values * scale).astype(jnp.bfloat16)
    for s in range(cap):
        pick = (member & (slot == s)).astype(jnp.bfloat16)
        rows = jnp.dot(pick, normed, preferred_element_type=jnp.float32)
        for j in range(chunks):
            wide[pl.ds(s * chunks + j, owners, stride=block), :] = rows[
                :, j * LANES : (j + 1) * LANES
            ]
    out_ref[...] = wide[...].astype(jnp.bfloat16)


def unpack(sources, cap, block_ref, wide, rows_ref):
    chunks = rows_ref.shape[1] // LANES
    block = cap * chunks + META
    wide[...] = block_ref[...].astype(jnp.float32)
    for s in range(cap):
        for j in range(chunks):
            rows_ref[s * sources : (s + 1) * sources, j * LANES : (j + 1) * LANES] = wide[
                pl.ds(s * chunks + j, sources, stride=block), :
            ].astype(jnp.bfloat16)
    digit = [wide[pl.ds(cap * chunks + r, sources, stride=block), :] for r in range(META)]
    middle = pltpu.roll(digit[0], LANES - SIDE, 1)
    return (digit[0] + 256.0 * middle + 65536.0 * digit[1]).astype(jnp.int32)


def best_of(sources, cap, keys_ref, key_value, queries_ref, query_value, best_ref):
    turned = query_value.T
    step = 2 if cap % 2 == 0 else 1
    for q in range(0, cap, step):
        queries = queries_ref[q * sources : (q + step) * sources, :]
        best = [best_ref[q + i : q + i + 1, :] for i in range(step)]
        for k in range(0, cap, step):
            scores = lax.dot_general(
                keys_ref[k * sources : (k + step) * sources, :],
                queries,
                (((1,), (1,)), ((), ())),
                preferred_element_type=jnp.float32,
            )
            for i in range(step):
                mine = turned[q + i : q + i + 1, :]
                floor = mine & ~(CLASS - 1)
                for m in range(step):
                    theirs = key_value[:, k + m : k + m + 1]
                    allowed = (theirs >= floor) & (theirs < mine)
                    part = scores[m * sources : (m + 1) * sources, i * sources : (i + 1) * sources]
                    top = jnp.max(jnp.where(allowed, part, -1.0), axis=0, keepdims=True)
                    best[i] = jnp.maximum(best[i], top)
        for i in range(step):
            best_ref[q + i : q + i + 1, :] = best[i]


def own_kernel(sources, cap, block_ref, rows_ref, value_ref, best_ref, wide):
    value = unpack(sources, cap, block_ref, wide, rows_ref)
    value_ref[...] = value
    best_ref[...] = jnp.full(best_ref.shape, -1.0, jnp.float32)
    best_of(sources, cap, rows_ref, value, rows_ref, value, best_ref)


def other_kernel(
    sources, cap, block_ref, own_ref, own_value_ref, own_best_ref, out_ref, wide, rows, best
):
    value = unpack(sources, cap, block_ref, wide, rows)
    best[...] = jnp.full(best.shape, -1.0, jnp.float32)
    best[: own_best_ref.shape[0], :] = own_best_ref[...]
    best_of(sources, cap, rows, value, own_ref, own_value_ref[...], best)
    out_ref[...] = best[...].T


def pick_kernel(owners, cap, cluster_ref, result_ref, out_ref):
    count = cluster_ref.shape[0]
    member, slot = routing(cluster_ref[...].reshape(1, count), owners)
    result = result_ref[...]
    found = jnp.full(slot.shape, -1.0, jnp.float32)
    for s in range(cap):
        here = jnp.max(
            jnp.where(member, result[:, s : s + 1], -2.0), axis=0, keepdims=True
        )
        found = jnp.where(slot == s, here, found)
    out_ref[...] = found.reshape(count)


def call(kernel, out_shape, scratch=(), in_specs=None):
    return pl.pallas_call(
        kernel,
        out_shape=out_shape,
        scratch_shapes=list(scratch),
        compiler_params=pltpu.CompilerParams(vmem_limit_bytes=VMEM_LIMIT),
        **({} if in_specs is None else {"in_specs": in_specs}),
    )


def per_device(embedding, cluster, member_order):
    owners = lax.axis_size("dp")
    count, feature = embedding.shape
    cap = max(2, 2 * count // owners)
    block = cap * feature // LANES + META
    shape = jax.ShapeDtypeStruct
    wide = pltpu.VMEM((owners * block, LANES), jnp.float32)
    packed = call(
        functools.partial(pack_kernel, owners, cap),
        shape((owners * block, LANES), jnp.bfloat16),
        [pltpu.VMEM(x.shape, x.dtype) for x in (cluster, member_order, embedding)]
        + [wide, pltpu.SemaphoreType.DMA((3,))],
        [pl.BlockSpec(memory_space=pltpu.HBM)] * 3,
    )(cluster, member_order, embedding)
    arrived = lax.all_to_all(
        packed.reshape(owners, block // 2, 2, LANES), "dp", split_axis=0, concat_axis=0, tiled=True
    ).reshape(owners * block, LANES)
    other = lax.ppermute(arrived, "helper", [(0, 1), (1, 0)])
    rows, value, best = call(
        functools.partial(own_kernel, owners, cap),
        (
            shape((owners * cap, feature), jnp.bfloat16),
            shape((owners, LANES), jnp.int32),
            shape((8, owners), jnp.float32),
        ),
        [wide],
    )(arrived)
    nearest = call(
        functools.partial(other_kernel, owners, cap),
        shape((owners, LANES), jnp.float32),
        [
            wide,
            pltpu.VMEM((owners * cap, feature), jnp.bfloat16),
            pltpu.VMEM((LANES, owners), jnp.float32),
        ],
    )(other, rows, value, best)
    returned = lax.all_to_all(
        nearest.reshape(owners, 1, LANES), "dp", split_axis=0, concat_axis=0, tiled=True
    ).reshape(owners, LANES)
    return call(functools.partial(pick_kernel, owners, cap), shape((count,), jnp.float32))(
        cluster, returned
    )


def solution(mesh):
    in_specs = (P(("dp", "helper"), None), P(("dp", "helper")), P(("dp", "helper")))
    out_specs = P(("dp", "helper"))
    return jax.shard_map(
        per_device, mesh=mesh, in_specs=in_specs, out_specs=out_specs, check_vma=False
    )
```

```python
import functools

import jax
import jax.numpy as jnp
from jax import lax
from jax.experimental import pallas as pl
from jax.experimental.pallas import tpu as pltpu
from jax.sharding import PartitionSpec as P

LANES = 128
META = 2
SIDE = 8
CLASS = 1 << 17
VMEM_LIMIT = 48 << 20


def routing(cluster, owners):
    count = cluster.shape[1]
    owner = lax.rem(cluster, owners)
    member = lax.broadcasted_iota(jnp.int32, (owners, count), 0) == owner
    before = lax.broadcasted_iota(jnp.int32, (count, count), 0) < lax.broadcasted_iota(
        jnp.int32, (count, count), 1
    )
    ones = member.astype(jnp.bfloat16)
    earlier = jnp.dot(ones, before.astype(jnp.bfloat16), preferred_element_type=jnp.float32)
    slot = jnp.sum(jnp.where(member, earlier, 0.0), axis=0, keepdims=True).astype(jnp.int32)
    return member, slot


def pack_kernel(
    owners, cap, cluster_hbm, order_hbm, x_hbm, out_ref, cluster_ref, order_ref, x_ref, wide, arrived
):
    given = (cluster_hbm, order_hbm, x_hbm)
    fetch = [
        pltpu.make_async_copy(source, target, arrived.at[i])
        for i, (source, target) in enumerate(zip(given, (cluster_ref, order_ref, x_ref)))
    ]
    for copy in fetch:
        copy.start()
    fetch[0].wait()
    fetch[1].wait()
    count, feature = x_ref.shape
    chunks = feature // LANES
    block = cap * chunks + META
    cluster = cluster_ref[...].reshape(1, count)
    order = order_ref[...].reshape(1, count)
    member, slot = routing(cluster, owners)
    ones = member.astype(jnp.bfloat16)
    lane = lax.broadcasted_iota(jnp.int32, (LANES, count), 0)
    low, middle = order & 255, (order >> 8) & 255
    high = (order >> 16) + 2 * lax.div(cluster, owners) + 8
    spread = (
        jnp.where(lane == slot, low, jnp.where(lane == slot + SIDE, middle, 0)),
        jnp.where(lane == slot, high, 0),
    )
    for r in range(META):
        wide[pl.ds(cap * chunks + r, owners, stride=block), :] = lax.dot_general(
            ones,
            spread[r].astype(jnp.float32).astype(jnp.bfloat16),
            (((1,), (1,)), ((), ())),
            preferred_element_type=jnp.float32,
        )
    fetch[2].wait()
    values = x_ref[...].astype(jnp.float32)
    scale = lax.rsqrt(jnp.sum(values * values, axis=1, keepdims=True) + 1e-06)
    normed = (values * scale).astype(jnp.bfloat16)
    for s in range(cap):
        pick = (member & (slot == s)).astype(jnp.bfloat16)
        rows = jnp.dot(pick, normed, preferred_element_type=jnp.float32)
        for j in range(chunks):
            wide[pl.ds(s * chunks + j, owners, stride=block), :] = rows[
                :, j * LANES : (j + 1) * LANES
            ]
    out_ref[...] = wide[...].astype(jnp.bfloat16)


def unpack(sources, cap, block_ref, wide, rows_ref):
    chunks = rows_ref.shape[1] // LANES
    block = cap * chunks + META
    wide[...] = block_ref[...].astype(jnp.float32)
    for s in range(cap):
        for j in range(chunks):
            rows_ref[s * sources : (s + 1) * sources, j * LANES : (j + 1) * LANES] = wide[
                pl.ds(s * chunks + j, sources, stride=block), :
            ].astype(jnp.bfloat16)
    digit = [wide[pl.ds(cap * chunks + r, sources, stride=block), :] for r in range(META)]
    middle = pltpu.roll(digit[0], LANES - SIDE, 1)
    return (digit[0] + 256.0 * middle + 65536.0 * digit[1]).astype(jnp.int32)


def best_of(sources, cap, keys_ref, key_value, queries_ref, query_value, best_ref):
    turned = query_value.T
    step = 2 if cap % 2 == 0 else 1
    for q in range(0, cap, step):
        queries = queries_ref[q * sources : (q + step) * sources, :]
        best = [best_ref[q + i : q + i + 1, :] for i in range(step)]
        for k in range(0, cap, step):
            scores = lax.dot_general(
                keys_ref[k * sources : (k + step) * sources, :],
                queries,
                (((1,), (1,)), ((), ())),
                preferred_element_type=jnp.float32,
            )
            for i in range(step):
                mine = turned[q + i : q + i + 1, :]
                floor = mine & ~(CLASS - 1)
                for m in range(step):
                    theirs = key_value[:, k + m : k + m + 1]
                    allowed = (theirs >= floor) & (theirs < mine)
                    part = scores[m * sources : (m + 1) * sources, i * sources : (i + 1) * sources]
                    top = jnp.max(jnp.where(allowed, part, -1.0), axis=0, keepdims=True)
                    best[i] = jnp.maximum(best[i], top)
        for i in range(step):
            best_ref[q + i : q + i + 1, :] = best[i]


def own_kernel(sources, cap, block_ref, rows_ref, value_ref, best_ref, wide):
    value = unpack(sources, cap, block_ref, wide, rows_ref)
    value_ref[...] = value
    best_ref[...] = jnp.full(best_ref.shape, -1.0, jnp.float32)
    best_of(sources, cap, rows_ref, value, rows_ref, value, best_ref)


def other_kernel(
    sources, cap, block_ref, own_ref, own_value_ref, own_best_ref, out_ref, wide, rows, best
):
    value = unpack(sources, cap, block_ref, wide, rows)
    best[...] = jnp.full(best.shape, -1.0, jnp.float32)
    best[: own_best_ref.shape[0], :] = own_best_ref[...]
    best_of(sources, cap, rows, value, own_ref, own_value_ref[...], best)
    out_ref[...] = best[...].T


def pick_kernel(owners, cap, cluster_ref, result_ref, out_ref):
    count = cluster_ref.shape[0]
    member, slot = routing(cluster_ref[...].reshape(1, count), owners)
    result = result_ref[...]
    found = jnp.full(slot.shape, -1.0, jnp.float32)
    for s in range(cap):
        here = jnp.max(
            jnp.where(member, result[:, s : s + 1], -2.0), axis=0, keepdims=True
        )
        found = jnp.where(slot == s, here, found)
    out_ref[...] = found.reshape(count)


def call(kernel, out_shape, scratch=(), in_specs=None):
    return pl.pallas_call(
        kernel,
        out_shape=out_shape,
        scratch_shapes=list(scratch),
        compiler_params=pltpu.CompilerParams(vmem_limit_bytes=VMEM_LIMIT),
        **({} if in_specs is None else {"in_specs": in_specs}),
    )


def per_device(embedding, cluster, member_order):
    owners = lax.axis_size("dp")
    count, feature = embedding.shape
    cap = max(2, 2 * count // owners)
    block = cap * feature // LANES + META
    shape = jax.ShapeDtypeStruct
    wide = pltpu.VMEM((owners * block, LANES), jnp.float32)
    packed = call(
        functools.partial(pack_kernel, owners, cap),
        shape((owners * block, LANES), jnp.bfloat16),
        [pltpu.VMEM(x.shape, x.dtype) for x in (cluster, member_order, embedding)]
        + [wide, pltpu.SemaphoreType.DMA((3,))],
        [pl.BlockSpec(memory_space=pltpu.HBM)] * 3,
    )(*(pltpu.with_memory_space_constraint(x, pltpu.HBM) for x in (cluster, member_order, embedding)))
    arrived = lax.all_to_all(
        packed.reshape(owners, block // 2, 2, LANES), "dp", split_axis=0, concat_axis=0, tiled=True
    ).reshape(owners * block, LANES)
    other = lax.ppermute(arrived, "helper", [(0, 1), (1, 0)])
    rows, value, best = call(
        functools.partial(own_kernel, owners, cap),
        (
            shape((owners * cap, feature), jnp.bfloat16),
            shape((owners, LANES), jnp.int32),
            shape((8, owners), jnp.float32),
        ),
        [wide],
    )(arrived)
    nearest = call(
        functools.partial(other_kernel, owners, cap),
        shape((owners, LANES), jnp.float32),
        [
            wide,
            pltpu.VMEM((owners * cap, feature), jnp.bfloat16),
            pltpu.VMEM((LANES, owners), jnp.float32),
        ],
    )(other, rows, value, best)
    returned = lax.all_to_all(
        nearest.reshape(owners, 1, LANES), "dp", split_axis=0, concat_axis=0, tiled=True
    ).reshape(owners, LANES)
    return call(functools.partial(pick_kernel, owners, cap), shape((count,), jnp.float32))(
        cluster, returned
    )


def solution(mesh):
    in_specs = (P(("dp", "helper"), None), P(("dp", "helper")), P(("dp", "helper")))
    out_specs = P(("dp", "helper"))
    return jax.shard_map(
        per_device, mesh=mesh, in_specs=in_specs, out_specs=out_specs, check_vma=False
    )
```

```python
import functools

import jax
import jax.numpy as jnp
from jax import lax
from jax.experimental import pallas as pl
from jax.experimental.pallas import tpu as pltpu
from jax.sharding import PartitionSpec as P

LANES = 128
META = 2
SIDE = 8
CLASS = 1 << 17
VMEM_LIMIT = 48 << 20
GRID = (4, 4, 8)


def chip_order(owners):
    opposite = 0
    for size in GRID:
        opposite = opposite * size + size // 2
    bits = owners.bit_length() - 1
    return [opposite ^ int(f"{i:0{bits}b}"[::-1], 2) for i in range(owners)]


def exchange(blocks, owners):
    return lax.all_to_all(
        blocks,
        "dp",
        split_axis=0,
        concat_axis=0,
        axis_index_groups=[chip_order(owners)],
        tiled=True,
    )


def routing(cluster, owners):
    count = cluster.shape[1]
    owner = lax.rem(cluster, owners)
    member = lax.broadcasted_iota(jnp.int32, (owners, count), 0) == owner
    before = lax.broadcasted_iota(jnp.int32, (count, count), 0) < lax.broadcasted_iota(
        jnp.int32, (count, count), 1
    )
    ones = member.astype(jnp.bfloat16)
    earlier = jnp.dot(ones, before.astype(jnp.bfloat16), preferred_element_type=jnp.float32)
    slot = jnp.sum(jnp.where(member, earlier, 0.0), axis=0, keepdims=True).astype(jnp.int32)
    return member, slot


def pack_kernel(
    owners, cap, cluster_hbm, order_hbm, x_hbm, out_ref, cluster_ref, order_ref, x_ref, wide, arrived
):
    given = (cluster_hbm, order_hbm, x_hbm)
    fetch = [
        pltpu.make_async_copy(source, target, arrived.at[i])
        for i, (source, target) in enumerate(zip(given, (cluster_ref, order_ref, x_ref)))
    ]
    for copy in fetch:
        copy.start()
    fetch[0].wait()
    fetch[1].wait()
    count, feature = x_ref.shape
    chunks = feature // LANES
    block = cap * chunks + META
    cluster = cluster_ref[...].reshape(1, count)
    order = order_ref[...].reshape(1, count)
    member, slot = routing(cluster, owners)
    ones = member.astype(jnp.bfloat16)
    lane = lax.broadcasted_iota(jnp.int32, (LANES, count), 0)
    low, middle = order & 255, (order >> 8) & 255
    high = (order >> 16) + 2 * lax.div(cluster, owners) + 8
    spread = (
        jnp.where(lane == slot, low, jnp.where(lane == slot + SIDE, middle, 0)),
        jnp.where(lane == slot, high, 0),
    )
    for r in range(META):
        wide[pl.ds(cap * chunks + r, owners, stride=block), :] = lax.dot_general(
            ones,
            spread[r].astype(jnp.float32).astype(jnp.bfloat16),
            (((1,), (1,)), ((), ())),
            preferred_element_type=jnp.float32,
        )
    picks = jnp.concatenate([member & (slot == s) for s in range(cap)], axis=0).astype(jnp.bfloat16)
    fetch[2].wait()
    values = x_ref[...].astype(jnp.float32)
    scale = lax.rsqrt(jnp.sum(values * values, axis=1, keepdims=True) + 1e-06)
    normed = (values * scale).astype(jnp.bfloat16)
    rows = jnp.dot(picks, normed, preferred_element_type=jnp.float32)
    for s in range(cap):
        for j in range(chunks):
            wide[pl.ds(s * chunks + j, owners, stride=block), :] = rows[
                s * owners : (s + 1) * owners, j * LANES : (j + 1) * LANES
            ]
    out_ref[...] = wide[...].astype(jnp.bfloat16)


def unpack(sources, cap, block_ref, wide, rows_ref):
    chunks = rows_ref.shape[1] // LANES
    block = cap * chunks + META
    wide[...] = block_ref[...].astype(jnp.float32)
    for s in range(cap):
        for j in range(chunks):
            rows_ref[s * sources : (s + 1) * sources, j * LANES : (j + 1) * LANES] = wide[
                pl.ds(s * chunks + j, sources, stride=block), :
            ].astype(jnp.bfloat16)
    digit = [wide[pl.ds(cap * chunks + r, sources, stride=block), :] for r in range(META)]
    middle = pltpu.roll(digit[0], LANES - SIDE, 1)
    return (digit[0] + 256.0 * middle + 65536.0 * digit[1]).astype(jnp.int32)


def best_of(cap, keys_ref, key_value, queries_ref, query_value, best_ref):
    turned = query_value.T
    sources, size = query_value.shape[0], key_value.shape[0]
    step = 2 if cap % 2 == 0 else 1
    for q in range(0, cap, step):
        scores = lax.dot_general(
            keys_ref[...],
            queries_ref[q * sources : (q + step) * sources, :],
            (((1,), (1,)), ((), ())),
            preferred_element_type=jnp.float32,
        )
        for i in range(step):
            mine = turned[q + i : q + i + 1, :]
            floor = mine & ~(CLASS - 1)
            best = best_ref[q + i : q + i + 1, :]
            for k in range(cap):
                theirs = key_value[:, k : k + 1]
                allowed = (theirs >= floor) & (theirs < mine)
                part = scores[k * size : (k + 1) * size, i * sources : (i + 1) * sources]
                top = jnp.max(jnp.where(allowed, part, -1.0), axis=0, keepdims=True)
                best = jnp.maximum(best, top)
            best_ref[q + i : q + i + 1, :] = best


def own_kernel(cap, block_ref, rows_ref, value_ref, best_ref, wide):
    value_ref[...] = unpack(value_ref.shape[0], cap, block_ref, wide, rows_ref)
    best_ref[...] = jnp.full(best_ref.shape, -1.0, jnp.float32)
    best_of(cap, rows_ref, value_ref[...], rows_ref, value_ref[...], best_ref)


def other_kernel(cap, block_ref, own_ref, own_value_ref, before_ref, out_ref, wide, rows, best):
    value = unpack(rows.shape[0] // cap, cap, block_ref, wide, rows)
    best[...] = jnp.full(best.shape, -1.0, jnp.float32)
    best[: before_ref.shape[0], :] = before_ref[...]
    best_of(cap, rows, value, own_ref, own_value_ref[...], best)
    out_ref[...] = best[...].T


def pick_kernel(owners, cap, cluster_ref, result_ref, out_ref):
    count = cluster_ref.shape[0]
    member, slot = routing(cluster_ref[...].reshape(1, count), owners)
    result = result_ref[...]
    found = jnp.full(slot.shape, -1.0, jnp.float32)
    for s in range(cap):
        here = jnp.max(
            jnp.where(member, result[:, s : s + 1], -2.0), axis=0, keepdims=True
        )
        found = jnp.where(slot == s, here, found)
    out_ref[...] = found.reshape(count)


def call(kernel, out_shape, scratch=(), in_specs=None):
    return pl.pallas_call(
        kernel,
        out_shape=out_shape,
        scratch_shapes=list(scratch),
        compiler_params=pltpu.CompilerParams(vmem_limit_bytes=VMEM_LIMIT),
        **({} if in_specs is None else {"in_specs": in_specs}),
    )


def per_device(embedding, cluster, member_order):
    owners = lax.axis_size("dp")
    count, feature = embedding.shape
    cap = max(2, 2 * count // owners)
    block = cap * feature // LANES + META
    shape = jax.ShapeDtypeStruct
    wide = pltpu.VMEM((owners * block, LANES), jnp.float32)
    packed = call(
        functools.partial(pack_kernel, owners, cap),
        shape((owners * block, LANES), jnp.bfloat16),
        [pltpu.VMEM(x.shape, x.dtype) for x in (cluster, member_order, embedding)]
        + [wide, pltpu.SemaphoreType.DMA((3,))],
        [pl.BlockSpec(memory_space=pltpu.HBM)] * 3,
    )(*(pltpu.with_memory_space_constraint(x, pltpu.HBM) for x in (cluster, member_order, embedding)))
    arrived = exchange(packed.reshape(owners, block // 2, 2, LANES), owners).reshape(
        owners * block, LANES
    )
    other = lax.ppermute(arrived, "helper", [(0, 1), (1, 0)])
    rows, value, best = call(
        functools.partial(own_kernel, cap),
        (
            shape((owners * cap, feature), jnp.bfloat16),
            shape((owners, LANES), jnp.int32),
            shape((8, owners), jnp.float32),
        ),
        [wide],
    )(arrived)
    nearest = call(
        functools.partial(other_kernel, cap),
        shape((owners, LANES), jnp.float32),
        [
            wide,
            pltpu.VMEM((owners * cap, feature), jnp.bfloat16),
            pltpu.VMEM((LANES, owners), jnp.float32),
        ],
    )(other, rows, value, best)
    returned = exchange(nearest.reshape(owners, 1, LANES), owners).reshape(owners, LANES)
    return call(functools.partial(pick_kernel, owners, cap), shape((count,), jnp.float32))(
        cluster, returned
    )


def solution(mesh):
    in_specs = (P(("dp", "helper"), None), P(("dp", "helper")), P(("dp", "helper")))
    out_specs = P(("dp", "helper"))
    return jax.shard_map(
        per_device, mesh=mesh, in_specs=in_specs, out_specs=out_specs, check_vma=False
    )
```

```python
import functools

import jax
import jax.numpy as jnp
from jax import lax
from jax.experimental import pallas as pl
from jax.experimental.pallas import tpu as pltpu
from jax.sharding import PartitionSpec as P

LANES = 128
META = 2
SIDE = 8
CLASS = 1 << 17
VMEM_LIMIT = 48 << 20
PARTS = (64, 64)
GRID = (4, 4, 8)


def chip_order(owners):
    opposite = 0
    for size in GRID:
        opposite = opposite * size + size // 2
    bits = owners.bit_length() - 1
    return [opposite ^ int(f"{i:0{bits}b}"[::-1], 2) for i in range(owners)]


def exchange(blocks, owners):
    return lax.all_to_all(
        blocks,
        "dp",
        split_axis=0,
        concat_axis=0,
        axis_index_groups=[chip_order(owners)],
        tiled=True,
    )


def routing(cluster, owners):
    count = cluster.shape[1]
    owner = lax.rem(cluster, owners)
    member = lax.broadcasted_iota(jnp.int32, (owners, count), 0) == owner
    before = lax.broadcasted_iota(jnp.int32, (count, count), 0) < lax.broadcasted_iota(
        jnp.int32, (count, count), 1
    )
    ones = member.astype(jnp.bfloat16)
    earlier = jnp.dot(ones, before.astype(jnp.bfloat16), preferred_element_type=jnp.float32)
    slot = jnp.sum(jnp.where(member, earlier, 0.0), axis=0, keepdims=True).astype(jnp.int32)
    return member, slot


def pack_kernel(
    owners, cap, cluster_hbm, order_hbm, x_hbm, out_ref, cluster_ref, order_ref, x_ref, wide, arrived
):
    given = (cluster_hbm, order_hbm, x_hbm)
    fetch = [
        pltpu.make_async_copy(source, target, arrived.at[i])
        for i, (source, target) in enumerate(zip(given, (cluster_ref, order_ref, x_ref)))
    ]
    for copy in fetch:
        copy.start()
    fetch[0].wait()
    fetch[1].wait()
    count, feature = x_ref.shape
    chunks = feature // LANES
    block = cap * chunks + META
    cluster = cluster_ref[...].reshape(1, count)
    order = order_ref[...].reshape(1, count)
    member, slot = routing(cluster, owners)
    ones = member.astype(jnp.bfloat16)
    lane = lax.broadcasted_iota(jnp.int32, (LANES, count), 0)
    low, middle = order & 255, (order >> 8) & 255
    high = (order >> 16) + 2 * lax.div(cluster, owners) + 8
    spread = (
        jnp.where(lane == slot, low, jnp.where(lane == slot + SIDE, middle, 0)),
        jnp.where(lane == slot, high, 0),
    )
    for r in range(META):
        wide[pl.ds(cap * chunks + r, owners, stride=block), :] = lax.dot_general(
            ones,
            spread[r].astype(jnp.float32).astype(jnp.bfloat16),
            (((1,), (1,)), ((), ())),
            preferred_element_type=jnp.float32,
        )
    picks = jnp.concatenate([member & (slot == s) for s in range(cap)], axis=0).astype(jnp.bfloat16)
    fetch[2].wait()
    values = x_ref[...].astype(jnp.float32)
    scale = lax.rsqrt(jnp.sum(values * values, axis=1, keepdims=True) + 1e-06)
    normed = (values * scale).astype(jnp.bfloat16)
    rows = jnp.dot(picks, normed, preferred_element_type=jnp.float32)
    for s in range(cap):
        for j in range(chunks):
            wide[pl.ds(s * chunks + j, owners, stride=block), :] = rows[
                s * owners : (s + 1) * owners, j * LANES : (j + 1) * LANES
            ]
    out_ref[...] = wide[...].astype(jnp.bfloat16)


def unpack(sources, cap, block_ref, wide, rows_ref):
    chunks = rows_ref.shape[1] // LANES
    block = cap * chunks + META
    wide[...] = block_ref[...].astype(jnp.float32)
    for s in range(cap):
        for j in range(chunks):
            rows_ref[s * sources : (s + 1) * sources, j * LANES : (j + 1) * LANES] = wide[
                pl.ds(s * chunks + j, sources, stride=block), :
            ].astype(jnp.bfloat16)
    digit = [wide[pl.ds(cap * chunks + r, sources, stride=block), :] for r in range(META)]
    middle = pltpu.roll(digit[0], LANES - SIDE, 1)
    return (digit[0] + 256.0 * middle + 65536.0 * digit[1]).astype(jnp.int32)


def best_of(cap, keys_ref, key_value, queries_ref, query_value, best_ref):
    turned = query_value.T
    sources, size = query_value.shape[0], key_value.shape[0]
    step = 2 if cap % 2 == 0 else 1
    for q in range(0, cap, step):
        scores = lax.dot_general(
            keys_ref[...],
            queries_ref[q * sources : (q + step) * sources, :],
            (((1,), (1,)), ((), ())),
            preferred_element_type=jnp.float32,
        )
        for i in range(step):
            mine = turned[q + i : q + i + 1, :]
            floor = mine & ~(CLASS - 1)
            best = best_ref[q + i : q + i + 1, :]
            for k in range(cap):
                theirs = key_value[:, k : k + 1]
                allowed = (theirs >= floor) & (theirs < mine)
                part = scores[k * size : (k + 1) * size, i * sources : (i + 1) * sources]
                top = jnp.max(jnp.where(allowed, part, -1.0), axis=0, keepdims=True)
                best = jnp.maximum(best, top)
            best_ref[q + i : q + i + 1, :] = best


def split_kernel(block_ref, *part_refs):
    start = 0
    for part_ref in part_refs:
        part_ref[...] = block_ref[start : start + part_ref.shape[0], :]
        start += part_ref.shape[0]


def own_kernel(cap, block_ref, rows_ref, value_ref, best_ref, wide):
    value_ref[...] = unpack(value_ref.shape[0], cap, block_ref, wide, rows_ref)
    best_ref[...] = jnp.full(best_ref.shape, -1.0, jnp.float32)
    best_of(cap, rows_ref, value_ref[...], rows_ref, value_ref[...], best_ref)


def other_kernel(last, cap, block_ref, own_ref, own_value_ref, before_ref, out_ref, wide, rows, best):
    value = unpack(rows.shape[0] // cap, cap, block_ref, wide, rows)
    best[...] = jnp.full(best.shape, -1.0, jnp.float32)
    best[: before_ref.shape[0], :] = before_ref[...]
    best_of(cap, rows, value, own_ref, own_value_ref[...], best)
    out_ref[...] = best[...].T if last else best[: out_ref.shape[0], :]


def pick_kernel(owners, cap, cluster_ref, result_ref, out_ref):
    count = cluster_ref.shape[0]
    member, slot = routing(cluster_ref[...].reshape(1, count), owners)
    result = result_ref[...]
    found = jnp.full(slot.shape, -1.0, jnp.float32)
    for s in range(cap):
        here = jnp.max(
            jnp.where(member, result[:, s : s + 1], -2.0), axis=0, keepdims=True
        )
        found = jnp.where(slot == s, here, found)
    out_ref[...] = found.reshape(count)


def call(kernel, out_shape, scratch=(), in_specs=None):
    return pl.pallas_call(
        kernel,
        out_shape=out_shape,
        scratch_shapes=list(scratch),
        compiler_params=pltpu.CompilerParams(vmem_limit_bytes=VMEM_LIMIT),
        **({} if in_specs is None else {"in_specs": in_specs}),
    )


def per_device(embedding, cluster, member_order):
    owners = lax.axis_size("dp")
    count, feature = embedding.shape
    cap = max(2, 2 * count // owners)
    block = cap * feature // LANES + META
    shape = jax.ShapeDtypeStruct
    wide = pltpu.VMEM((owners * block, LANES), jnp.float32)
    packed = call(
        functools.partial(pack_kernel, owners, cap),
        shape((owners * block, LANES), jnp.bfloat16),
        [pltpu.VMEM(x.shape, x.dtype) for x in (cluster, member_order, embedding)]
        + [wide, pltpu.SemaphoreType.DMA((3,))],
        [pl.BlockSpec(memory_space=pltpu.HBM)] * 3,
    )(*(pltpu.with_memory_space_constraint(x, pltpu.HBM) for x in (cluster, member_order, embedding)))
    arrived = exchange(packed.reshape(owners, block // 2, 2, LANES), owners).reshape(
        owners * block, LANES
    )
    parts = [shape((size * block, LANES), jnp.bfloat16) for size in PARTS]
    others = [
        lax.ppermute(rows, "helper", [(0, 1), (1, 0)]) for rows in call(split_kernel, parts)(arrived)
    ]
    rows, value, best = call(
        functools.partial(own_kernel, cap),
        (
            shape((owners * cap, feature), jnp.bfloat16),
            shape((owners, LANES), jnp.int32),
            shape((8, owners), jnp.float32),
        ),
        [wide],
    )(arrived)
    for p, (size, other) in enumerate(zip(PARTS, others)):
        last = p == len(PARTS) - 1
        best = call(
            functools.partial(other_kernel, last, cap),
            shape((owners, LANES) if last else (8, owners), jnp.float32),
            [
                pltpu.VMEM((size * block, LANES), jnp.float32),
                pltpu.VMEM((size * cap, feature), jnp.bfloat16),
                pltpu.VMEM((LANES, owners), jnp.float32),
            ],
        )(other, rows, value, best)
    returned = exchange(best.reshape(owners, 1, LANES), owners).reshape(owners, LANES)
    return call(functools.partial(pick_kernel, owners, cap), shape((count,), jnp.float32))(
        cluster, returned
    )


def solution(mesh):
    in_specs = (P(("dp", "helper"), None), P(("dp", "helper")), P(("dp", "helper")))
    out_specs = P(("dp", "helper"))
    return jax.shard_map(
        per_device, mesh=mesh, in_specs=in_specs, out_specs=out_specs, check_vma=False
    )
```

```python
import functools

import jax
import jax.numpy as jnp
from jax import lax
from jax.experimental import pallas as pl
from jax.experimental.pallas import tpu as pltpu
from jax.sharding import PartitionSpec as P

LANES = 128
META = 2
SIDE = 8
CLASS = 1 << 17
VMEM_LIMIT = 48 << 20
PARTS = (64, 64)
GRID = (4, 4, 8)


def chip_order(owners):
    opposite = 0
    for size in GRID:
        opposite = opposite * size + size // 2
    bits = owners.bit_length() - 1
    return [opposite ^ int(f"{i:0{bits}b}"[::-1], 2) for i in range(owners)]


def exchange(blocks, owners):
    return lax.all_to_all(
        blocks,
        "dp",
        split_axis=0,
        concat_axis=0,
        axis_index_groups=[chip_order(owners)],
        tiled=True,
    )


def earlier_documents(count):
    row = lax.broadcasted_iota(jnp.int32, (count, count), 0)
    return (row < lax.broadcasted_iota(jnp.int32, (count, count), 1)).astype(jnp.bfloat16)


def routing(cluster, owners, before):
    count = cluster.shape[1]
    owner = lax.rem(cluster, owners)
    member = lax.broadcasted_iota(jnp.int32, (owners, count), 0) == owner
    ones = member.astype(jnp.bfloat16)
    earlier = jnp.dot(ones, before, preferred_element_type=jnp.float32)
    slot = jnp.sum(jnp.where(member, earlier, 0.0), axis=0, keepdims=True).astype(jnp.int32)
    return member, slot


def pack_kernel(
    owners, cap, cluster_hbm, order_hbm, x_hbm, out_ref, place_ref, cluster_ref, order_ref, x_ref, wide, arrived
):
    given = (cluster_hbm, order_hbm, x_hbm)
    fetch = [
        pltpu.make_async_copy(source, target, arrived.at[i])
        for i, (source, target) in enumerate(zip(given, (cluster_ref, order_ref, x_ref)))
    ]
    for copy in fetch:
        copy.start()
    count, feature = x_ref.shape
    before = earlier_documents(count)
    fetch[0].wait()
    chunks = feature // LANES
    block = cap * chunks + META
    cluster = cluster_ref[...].reshape(1, count)
    member, slot = routing(cluster, owners, before)
    place_ref[0:1, :] = lax.rem(cluster, owners)
    place_ref[1:2, :] = slot
    ones = member.astype(jnp.bfloat16)
    lane = lax.broadcasted_iota(jnp.int32, (LANES, count), 0)
    fetch[1].wait()
    order = order_ref[...].reshape(1, count)
    low, middle = order & 255, (order >> 8) & 255
    high = (order >> 16) + 2 * lax.div(cluster, owners) + 8
    spread = (
        jnp.where(lane == slot, low, jnp.where(lane == slot + SIDE, middle, 0)),
        jnp.where(lane == slot, high, 0),
    )
    for r in range(META):
        wide[pl.ds(cap * chunks + r, owners, stride=block), :] = lax.dot_general(
            ones,
            spread[r].astype(jnp.float32).astype(jnp.bfloat16),
            (((1,), (1,)), ((), ())),
            preferred_element_type=jnp.float32,
        )
    picks = jnp.concatenate([member & (slot == s) for s in range(cap)], axis=0).astype(jnp.bfloat16)
    fetch[2].wait()
    values = x_ref[...].astype(jnp.float32)
    scale = lax.rsqrt(jnp.sum(values * values, axis=1, keepdims=True) + 1e-06)
    normed = (values * scale).astype(jnp.bfloat16)
    rows = jnp.dot(picks, normed, preferred_element_type=jnp.float32)
    for s in range(cap):
        for j in range(chunks):
            wide[pl.ds(s * chunks + j, owners, stride=block), :] = rows[
                s * owners : (s + 1) * owners, j * LANES : (j + 1) * LANES
            ]
    out_ref[...] = wide[...].astype(jnp.bfloat16)


def unpack(sources, cap, block_ref, wide, rows_ref):
    chunks = rows_ref.shape[1] // LANES
    block = cap * chunks + META
    wide[...] = block_ref[...].astype(jnp.float32)
    for s in range(cap):
        for j in range(chunks):
            rows_ref[s * sources : (s + 1) * sources, j * LANES : (j + 1) * LANES] = wide[
                pl.ds(s * chunks + j, sources, stride=block), :
            ].astype(jnp.bfloat16)
    digit = [wide[pl.ds(cap * chunks + r, sources, stride=block), :] for r in range(META)]
    middle = pltpu.roll(digit[0], LANES - SIDE, 1)
    return (digit[0] + 256.0 * middle + 65536.0 * digit[1]).astype(jnp.int32)


def best_of(cap, keys_ref, key_value, queries_ref, query_value, best_ref):
    turned = query_value.T
    sources, size = query_value.shape[0], key_value.shape[0]
    step = 2 if cap % 2 == 0 else 1
    for q in range(0, cap, step):
        scores = lax.dot_general(
            keys_ref[...],
            queries_ref[q * sources : (q + step) * sources, :],
            (((1,), (1,)), ((), ())),
            preferred_element_type=jnp.float32,
        )
        for i in range(step):
            mine = turned[q + i : q + i + 1, :]
            floor = mine & ~(CLASS - 1)
            best = best_ref[q + i : q + i + 1, :]
            for k in range(cap):
                theirs = key_value[:, k : k + 1]
                allowed = (theirs >= floor) & (theirs < mine)
                part = scores[k * size : (k + 1) * size, i * sources : (i + 1) * sources]
                top = jnp.max(jnp.where(allowed, part, -1.0), axis=0, keepdims=True)
                best = jnp.maximum(best, top)
            best_ref[q + i : q + i + 1, :] = best


def best_among(cap, rows_ref, value, best_ref):
    sources = value.shape[0]
    turned = value.T
    step = 2 if cap % 2 == 0 else 1
    down = [jnp.broadcast_to(value[:, k : k + 1], (sources, sources)) for k in range(cap)]
    across = [jnp.full((1, sources), -1.0, jnp.float32) for _ in range(cap)]
    along = [None] * cap
    for q in range(0, cap, step):
        for k in range(0, q + 1, step):
            scores = lax.dot_general(
                rows_ref[k * sources : (k + step) * sources, :],
                rows_ref[q * sources : (q + step) * sources, :],
                (((1,), (1,)), ((), ())),
                preferred_element_type=jnp.float32,
            )
            for i in range(q, q + step):
                mine = turned[i : i + 1, :]
                for m in range(k, k + step):
                    theirs = down[m]
                    part = scores[
                        (m - k) * sources : (m - k + 1) * sources,
                        (i - q) * sources : (i - q + 1) * sources,
                    ]
                    allowed = (theirs >= (mine & ~(CLASS - 1))) & (theirs < mine)
                    top = jnp.max(jnp.where(allowed, part, -1.0), axis=0, keepdims=True)
                    across[i] = jnp.maximum(across[i], top)
                    if k < q:
                        allowed = (mine >= (theirs & ~(CLASS - 1))) & (mine < theirs)
                        top = jnp.where(allowed, part, -1.0)
                        along[m] = top if along[m] is None else jnp.maximum(along[m], top)
    lane = lax.broadcasted_iota(jnp.int32, (sources, LANES), 1)
    columns = jnp.full((sources, LANES), -1.0, jnp.float32)
    for m, top in enumerate(along):
        if top is not None:
            columns = jnp.where(lane == m, jnp.max(top, axis=1, keepdims=True), columns)
    best_ref[...] = columns.T[: best_ref.shape[0], :]
    for i in range(cap):
        best_ref[i : i + 1, :] = jnp.maximum(best_ref[i : i + 1, :], across[i])


def split_kernel(block_ref, *part_refs):
    start = 0
    for part_ref in part_refs:
        part_ref[...] = block_ref[start : start + part_ref.shape[0], :]
        start += part_ref.shape[0]


def own_kernel(cap, block_ref, rows_ref, value_ref, best_ref, wide):
    value_ref[...] = unpack(value_ref.shape[0], cap, block_ref, wide, rows_ref)
    best_among(cap, rows_ref, value_ref[...], best_ref)


def other_kernel(last, cap, block_ref, own_ref, own_value_ref, before_ref, out_ref, wide, rows, best):
    value = unpack(rows.shape[0] // cap, cap, block_ref, wide, rows)
    best[...] = jnp.full(best.shape, -1.0, jnp.float32)
    best[: before_ref.shape[0], :] = before_ref[...]
    best_of(cap, rows, value, own_ref, own_value_ref[...], best)
    out_ref[...] = best[...].T if last else best[: out_ref.shape[0], :]


def pick_kernel(owners, cap, place_ref, result_ref, out_ref):
    count = place_ref.shape[1]
    member = lax.broadcasted_iota(jnp.int32, (owners, count), 0) == place_ref[0:1, :]
    slot = place_ref[1:2, :]
    result = result_ref[...]
    found = jnp.full(slot.shape, -1.0, jnp.float32)
    for s in range(cap):
        here = jnp.max(
            jnp.where(member, result[:, s : s + 1], -2.0), axis=0, keepdims=True
        )
        found = jnp.where(slot == s, here, found)
    out_ref[...] = found.reshape(count)


def call(kernel, out_shape, scratch=(), in_specs=None):
    return pl.pallas_call(
        kernel,
        out_shape=out_shape,
        scratch_shapes=list(scratch),
        compiler_params=pltpu.CompilerParams(vmem_limit_bytes=VMEM_LIMIT),
        **({} if in_specs is None else {"in_specs": in_specs}),
    )


def per_device(embedding, cluster, member_order):
    owners = lax.axis_size("dp")
    count, feature = embedding.shape
    cap = max(2, 2 * count // owners)
    block = cap * feature // LANES + META
    shape = jax.ShapeDtypeStruct
    wide = pltpu.VMEM((owners * block, LANES), jnp.float32)
    packed, place = call(
        functools.partial(pack_kernel, owners, cap),
        (shape((owners * block, LANES), jnp.bfloat16), shape((8, count), jnp.int32)),
        [pltpu.VMEM(x.shape, x.dtype) for x in (cluster, member_order, embedding)]
        + [wide, pltpu.SemaphoreType.DMA((3,))],
        [pl.BlockSpec(memory_space=pltpu.HBM)] * 3,
    )(*(pltpu.with_memory_space_constraint(x, pltpu.HBM) for x in (cluster, member_order, embedding)))
    arrived = exchange(packed.reshape(owners, block // 2, 2, LANES), owners).reshape(
        owners * block, LANES
    )
    parts = [shape((size * block, LANES), jnp.bfloat16) for size in PARTS]
    others = [
        lax.ppermute(rows, "helper", [(0, 1), (1, 0)]) for rows in call(split_kernel, parts)(arrived)
    ]
    rows, value, best = call(
        functools.partial(own_kernel, cap),
        (
            shape((owners * cap, feature), jnp.bfloat16),
            shape((owners, LANES), jnp.int32),
            shape((8, owners), jnp.float32),
        ),
        [wide],
    )(arrived)
    for p, (size, other) in enumerate(zip(PARTS, others)):
        last = p == len(PARTS) - 1
        best = call(
            functools.partial(other_kernel, last, cap),
            shape((owners, LANES) if last else (8, owners), jnp.float32),
            [
                pltpu.VMEM((size * block, LANES), jnp.float32),
                pltpu.VMEM((size * cap, feature), jnp.bfloat16),
                pltpu.VMEM((LANES, owners), jnp.float32),
            ],
        )(other, rows, value, best)
    returned = exchange(best.reshape(owners, 1, LANES), owners).reshape(owners, LANES)
    return call(functools.partial(pick_kernel, owners, cap), shape((count,), jnp.float32))(
        place, returned
    )


def solution(mesh):
    in_specs = (P(("dp", "helper"), None), P(("dp", "helper")), P(("dp", "helper")))
    out_specs = P(("dp", "helper"))
    return jax.shard_map(
        per_device, mesh=mesh, in_specs=in_specs, out_specs=out_specs, check_vma=False
    )
```

```python
import functools

import jax
import jax.numpy as jnp
from jax import lax
from jax.experimental import pallas as pl
from jax.experimental.pallas import tpu as pltpu
from jax.sharding import PartitionSpec as P

LANES = 128
META = 2
SIDE = 8
CLASS = 1 << 17
VMEM_LIMIT = 48 << 20
PARTS = (64, 64)
GRID = (4, 4, 8)


def chip_order(owners):
    opposite = 0
    for size in GRID:
        opposite = opposite * size + size // 2
    bits = owners.bit_length() - 1
    return [opposite ^ int(f"{i:0{bits}b}"[::-1], 2) for i in range(owners)]


def exchange(blocks, owners):
    return lax.all_to_all(
        blocks,
        "dp",
        split_axis=0,
        concat_axis=0,
        axis_index_groups=[chip_order(owners)],
        tiled=True,
    )


def earlier_documents(count):
    row = lax.broadcasted_iota(jnp.int32, (count, count), 0)
    return (row < lax.broadcasted_iota(jnp.int32, (count, count), 1)).astype(jnp.bfloat16)


def routing(cluster, owners, before):
    count = cluster.shape[1]
    owner = lax.rem(cluster, owners)
    member = lax.broadcasted_iota(jnp.int32, (owners, count), 0) == owner
    ones = member.astype(jnp.bfloat16)
    earlier = jnp.dot(ones, before, preferred_element_type=jnp.float32)
    slot = jnp.sum(jnp.where(member, earlier, 0.0), axis=0, keepdims=True).astype(jnp.int32)
    return member, slot


def pack_kernel(
    owners, cap, cluster_hbm, order_hbm, x_hbm, out_ref, place_ref, cluster_ref, order_ref, x_ref, wide, arrived
):
    given = (cluster_hbm, order_hbm, x_hbm)
    fetch = [
        pltpu.make_async_copy(source, target, arrived.at[i])
        for i, (source, target) in enumerate(zip(given, (cluster_ref, order_ref, x_ref)))
    ]
    for copy in fetch:
        copy.start()
    count, feature = x_ref.shape
    before = earlier_documents(count)
    fetch[0].wait()
    chunks = feature // LANES
    block = cap * chunks + META
    cluster = cluster_ref[...].reshape(1, count)
    member, slot = routing(cluster, owners, before)
    place_ref[0:1, :] = lax.rem(cluster, owners)
    place_ref[1:2, :] = slot
    ones = member.astype(jnp.bfloat16)
    lane = lax.broadcasted_iota(jnp.int32, (LANES, count), 0)
    fetch[1].wait()
    order = order_ref[...].reshape(1, count)
    low, middle = order & 255, (order >> 8) & 255
    high = (order >> 16) + 2 * lax.div(cluster, owners) + 8
    spread = (
        jnp.where(lane == slot, low, jnp.where(lane == slot + SIDE, middle, 0)),
        jnp.where(lane == slot, high, 0),
    )
    digits = lax.dot_general(
        ones,
        jnp.concatenate(spread, axis=0).astype(jnp.float32).astype(jnp.bfloat16),
        (((1,), (1,)), ((), ())),
        preferred_element_type=jnp.float32,
    )
    for r in range(META):
        wide[pl.ds(cap * chunks + r, owners, stride=block), :] = digits[
            :, r * LANES : (r + 1) * LANES
        ]
    picks = jnp.concatenate([member & (slot == s) for s in range(cap)], axis=0).astype(jnp.bfloat16)
    fetch[2].wait()
    values = x_ref[...].astype(jnp.float32)
    scale = lax.rsqrt(jnp.sum(values * values, axis=1, keepdims=True) + 1e-06)
    normed = (values * scale).astype(jnp.bfloat16)
    rows = jnp.dot(picks, normed, preferred_element_type=jnp.float32)
    for s in range(cap):
        for j in range(chunks):
            wide[pl.ds(s * chunks + j, owners, stride=block), :] = rows[
                s * owners : (s + 1) * owners, j * LANES : (j + 1) * LANES
            ]
    out_ref[...] = wide[...].astype(jnp.bfloat16)


def unpack(sources, cap, block_ref, wide, rows_ref):
    chunks = rows_ref.shape[1] // LANES
    block = cap * chunks + META
    wide[...] = block_ref[...].astype(jnp.float32)
    for s in range(cap):
        for j in range(chunks):
            rows_ref[s * sources : (s + 1) * sources, j * LANES : (j + 1) * LANES] = wide[
                pl.ds(s * chunks + j, sources, stride=block), :
            ].astype(jnp.bfloat16)
    digit = [wide[pl.ds(cap * chunks + r, sources, stride=block), :] for r in range(META)]
    middle = pltpu.roll(digit[0], LANES - SIDE, 1)
    return (digit[0] + 256.0 * middle + 65536.0 * digit[1]).astype(jnp.int32)


def best_of(cap, keys_ref, key_value, queries_ref, query_value, best_ref):
    turned = query_value.T
    sources, size = query_value.shape[0], key_value.shape[0]
    step = 2 if cap % 2 == 0 else 1
    for q in range(0, cap, step):
        scores = lax.dot_general(
            keys_ref[...],
            queries_ref[q * sources : (q + step) * sources, :],
            (((1,), (1,)), ((), ())),
            preferred_element_type=jnp.float32,
        )
        for i in range(step):
            mine = turned[q + i : q + i + 1, :]
            floor = mine & ~(CLASS - 1)
            best = best_ref[q + i : q + i + 1, :]
            for k in range(cap):
                theirs = key_value[:, k : k + 1]
                allowed = (theirs >= floor) & (theirs < mine)
                part = scores[k * size : (k + 1) * size, i * sources : (i + 1) * sources]
                top = jnp.max(jnp.where(allowed, part, -1.0), axis=0, keepdims=True)
                best = jnp.maximum(best, top)
            best_ref[q + i : q + i + 1, :] = best


def best_among(cap, rows_ref, value, best_ref):
    sources = value.shape[0]
    turned = value.T
    step = 2 if cap % 2 == 0 else 1
    down = [jnp.broadcast_to(value[:, k : k + 1], (sources, sources)) for k in range(cap)]
    across = [jnp.full((1, sources), -1.0, jnp.float32) for _ in range(cap)]
    along = [None] * cap
    for q in range(0, cap, step):
        for k in range(0, q + 1, step):
            scores = lax.dot_general(
                rows_ref[k * sources : (k + step) * sources, :],
                rows_ref[q * sources : (q + step) * sources, :],
                (((1,), (1,)), ((), ())),
                preferred_element_type=jnp.float32,
            )
            for i in range(q, q + step):
                mine = turned[i : i + 1, :]
                for m in range(k, k + step):
                    theirs = down[m]
                    part = scores[
                        (m - k) * sources : (m - k + 1) * sources,
                        (i - q) * sources : (i - q + 1) * sources,
                    ]
                    allowed = (theirs >= (mine & ~(CLASS - 1))) & (theirs < mine)
                    top = jnp.max(jnp.where(allowed, part, -1.0), axis=0, keepdims=True)
                    across[i] = jnp.maximum(across[i], top)
                    if k < q:
                        allowed = (mine >= (theirs & ~(CLASS - 1))) & (mine < theirs)
                        top = jnp.where(allowed, part, -1.0)
                        along[m] = top if along[m] is None else jnp.maximum(along[m], top)
    lane = lax.broadcasted_iota(jnp.int32, (sources, LANES), 1)
    columns = jnp.full((sources, LANES), -1.0, jnp.float32)
    for m, top in enumerate(along):
        if top is not None:
            columns = jnp.where(lane == m, jnp.max(top, axis=1, keepdims=True), columns)
    best_ref[...] = columns.T[: best_ref.shape[0], :]
    for i in range(cap):
        best_ref[i : i + 1, :] = jnp.maximum(best_ref[i : i + 1, :], across[i])


def split_kernel(block_ref, *part_refs):
    start = 0
    for part_ref in part_refs:
        part_ref[...] = block_ref[start : start + part_ref.shape[0], :]
        start += part_ref.shape[0]


def own_kernel(cap, block_ref, rows_ref, value_ref, best_ref, wide):
    value_ref[...] = unpack(value_ref.shape[0], cap, block_ref, wide, rows_ref)
    best_among(cap, rows_ref, value_ref[...], best_ref)


def other_kernel(last, cap, block_ref, own_ref, own_value_ref, before_ref, out_ref, wide, rows, best):
    value = unpack(rows.shape[0] // cap, cap, block_ref, wide, rows)
    best[...] = jnp.full(best.shape, -1.0, jnp.float32)
    best[: before_ref.shape[0], :] = before_ref[...]
    best_of(cap, rows, value, own_ref, own_value_ref[...], best)
    out_ref[...] = best[...].T if last else best[: out_ref.shape[0], :]


def pick_kernel(owners, cap, place_ref, result_ref, out_ref):
    count = place_ref.shape[1]
    member = lax.broadcasted_iota(jnp.int32, (owners, count), 0) == place_ref[0:1, :]
    slot = place_ref[1:2, :]
    result = result_ref[...]
    found = jnp.full(slot.shape, -1.0, jnp.float32)
    for s in range(cap):
        here = jnp.max(
            jnp.where(member, result[:, s : s + 1], -2.0), axis=0, keepdims=True
        )
        found = jnp.where(slot == s, here, found)
    out_ref[...] = found.reshape(count)


def call(kernel, out_shape, scratch=(), in_specs=None):
    return pl.pallas_call(
        kernel,
        out_shape=out_shape,
        scratch_shapes=list(scratch),
        compiler_params=pltpu.CompilerParams(vmem_limit_bytes=VMEM_LIMIT),
        **({} if in_specs is None else {"in_specs": in_specs}),
    )


def per_device(embedding, cluster, member_order):
    owners = lax.axis_size("dp")
    count, feature = embedding.shape
    cap = max(2, 2 * count // owners)
    block = cap * feature // LANES + META
    shape = jax.ShapeDtypeStruct
    wide = pltpu.VMEM((owners * block, LANES), jnp.float32)
    packed, place = call(
        functools.partial(pack_kernel, owners, cap),
        (shape((owners * block, LANES), jnp.bfloat16), shape((8, count), jnp.int32)),
        [pltpu.VMEM(x.shape, x.dtype) for x in (cluster, member_order, embedding)]
        + [wide, pltpu.SemaphoreType.DMA((3,))],
        [pl.BlockSpec(memory_space=pltpu.HBM)] * 3,
    )(*(pltpu.with_memory_space_constraint(x, pltpu.HBM) for x in (cluster, member_order, embedding)))
    arrived = exchange(packed.reshape(owners, block // 2, 2, LANES), owners).reshape(
        owners * block, LANES
    )
    parts = [shape((size * block, LANES), jnp.bfloat16) for size in PARTS]
    others = [
        lax.ppermute(rows, "helper", [(0, 1), (1, 0)]) for rows in call(split_kernel, parts)(arrived)
    ]
    rows, value, best = call(
        functools.partial(own_kernel, cap),
        (
            shape((owners * cap, feature), jnp.bfloat16),
            shape((owners, LANES), jnp.int32),
            shape((8, owners), jnp.float32),
        ),
        [wide],
    )(arrived)
    for p, (size, other) in enumerate(zip(PARTS, others)):
        last = p == len(PARTS) - 1
        best = call(
            functools.partial(other_kernel, last, cap),
            shape((owners, LANES) if last else (8, owners), jnp.float32),
            [
                pltpu.VMEM((size * block, LANES), jnp.float32),
                pltpu.VMEM((size * cap, feature), jnp.bfloat16),
                pltpu.VMEM((LANES, owners), jnp.float32),
            ],
        )(other, rows, value, best)
    returned = exchange(best.reshape(owners, 1, LANES), owners).reshape(owners, LANES)
    return call(functools.partial(pick_kernel, owners, cap), shape((count,), jnp.float32))(
        place, returned
    )


def solution(mesh):
    in_specs = (P(("dp", "helper"), None), P(("dp", "helper")), P(("dp", "helper")))
    out_specs = P(("dp", "helper"))
    return jax.shard_map(
        per_device, mesh=mesh, in_specs=in_specs, out_specs=out_specs, check_vma=False
    )
```
